32 devices in a mesh: chan: 8 (over z, y), ctr: 4 (over x, core).
Axes of the slice: x: 2, y: 2, z: 4, core: 2. Of those that a mesh axis runs over, the one named last changes fastest.
Arguments:
- amplitudes: float32 [4608, 8, 256], P('ctr', 'chan'), may hold values from -6 to 6
- pair_interaction: bfloat16 [8, 4608, 4608], P('chan', None, 'ctr'), may hold values from -0.09375 to 0.09375
- ph_interaction: float32 [16, 128, 128], P('chan'), may hold values from -0.5 to 0.5
- pp_size: int32 [8], P('chan'), may hold values from 1 to 72, as said below
- ph_owner: int32 [72, 8, 2], P('ctr', 'chan'), may hold values from 0 to 15, as said below
Outputs:
- residual: float32 [4608, 8, 256], P('ctr', 'chan')
The draws below stay inside these ranges and needn't reach their ends.
Inputs may be any that keep to these rules, and one draw needn't show every extreme that they name: Channel c has its first 64 * pp_size[c] particle pairs live; every draw has a channel with 72 live tiles. `ph_owner`: the ph channel g is owned by index g // 2 of chan. Of the 36 tiles that one device holds, at most 9 have ph channels owned by one index of chan; in every draw some index of chan receives exactly 9 tiles from every device.
All inputs are finite; a program needn't handle non-finite values.
Results may differ from the reference program's by a relative error of at most 0.002.
Values may be sent and summed in bfloat16 or wider, within the bound.
A program may use at most 128 MiB of HBM per device.

```python
import jax
import jax.numpy as jnp
from jax import lax

TS = 64
TC = 128
K = 4608
HP = 256
PH_DEV = 2
CH_DEV = 1
CHANNELS = 8
PH = 16
RT = 72
TILES_DEV = 36
CAP = 9
N_CHAN = 8
N_CTR = 4


def draw_pp_size(key, part):
    counts = jax.random.randint(jax.random.fold_in(key, 11), (CHANNELS,), 1, RT + 1)
    picked = jax.random.randint(jax.random.fold_in(key, 12), (2,), 0, CHANNELS)
    places = jnp.arange(CHANNELS)
    counts = jnp.where(places == picked[0], RT, counts)
    counts = jnp.where((places == picked[1]) & (picked[1] != picked[0]), 1, counts)
    return counts.astype(jnp.int32)


def draw_ph_owner(key, part):
    slot_total = N_CHAN * CAP
    owner_zero = jax.random.randint(jax.random.fold_in(key, 21), (), 0, N_CHAN)

    def per_device(device_key):
        slot_order = jax.random.permutation(jax.random.fold_in(device_key, 1), slot_total)
        target = slot_order // CAP
        scores = jnp.where(target == owner_zero, 0, slot_total) + jnp.arange(slot_total)
        ranked = slot_order[jnp.argsort(scores)]
        chosen = ranked[:TILES_DEV]
        chosen = chosen[jax.random.permutation(jax.random.fold_in(device_key, 2), TILES_DEV)]
        within = jax.random.randint(jax.random.fold_in(device_key, 3), (TILES_DEV,), 0, PH_DEV)
        return chosen // CAP * PH_DEV + within
    device_keys = jax.random.split(jax.random.fold_in(key, 22), N_CTR * N_CHAN)
    values_all = jax.vmap(per_device)(device_keys)
    values_all = values_all.reshape(N_CTR, N_CHAN, RT // N_CTR, CH_DEV, HP // TC)
    values_all = jnp.transpose(values_all, (0, 2, 1, 3, 4)).reshape(RT, CHANNELS, HP // TC)
    return values_all.astype(jnp.int32)


def block_scale(stream_key, dims, shards, low, largest):
    def one(axis_at, parts):
        heights = jax.random.uniform(jax.random.fold_in(jax.random.fold_in(stream_key, 6), axis_at), (parts,), jnp.float32, low / len(shards), largest / len(shards))
        return jnp.repeat(jnp.exp(heights), dims[axis_at] // parts).reshape((-1,) + (1,) * (len(dims) - axis_at - 1))

    factor_of = one(*shards[0])
    for cut in shards[1:]:
        factor_of = factor_of * one(*cut)
    return factor_of


def gaussian(stream_key, dims, deviation, limit, cuts=(), held_as=jnp.bfloat16):
    result = deviation * jax.random.normal(stream_key, dims, jnp.float32)
    if cuts:
        result = result * block_scale(stream_key, dims, cuts, -0.22, 0.18)
    return jnp.clip(result, -limit, limit).astype(held_as)


def setup_inputs(seed: int = 0) -> dict:
    key_list = jax.random.split(jax.random.key(seed), 6)
    amplitudes = gaussian(key_list[0], (K, CHANNELS, HP), 1.0, 6.0, ((0, 4), (1, 8)), jnp.float32)
    pair_interaction = gaussian(key_list[1], (CHANNELS, K, K), K ** -0.5, 0.09375, ((0, 8), (2, 4)))
    ph_interaction = gaussian(key_list[2], (PH, TC, TC), TC ** -0.5, 0.5, ((0, 8),), jnp.float32)
    pp_size = draw_pp_size(jax.random.fold_in(key_list[5], 71), 0)
    ph_owner = draw_ph_owner(jax.random.fold_in(key_list[5], 71), 0)
    return dict(amplitudes=amplitudes, pair_interaction=pair_interaction, ph_interaction=ph_interaction, pp_size=pp_size, ph_owner=ph_owner)


def reference(amplitudes, pair_interaction, ph_interaction, pp_size, ph_owner):
    positions = jnp.arange(K, dtype=jnp.int32)
    live_mask = positions[:, None] < (pp_size * TS)[None, :]
    masked = jnp.where(live_mask[:, :, None], amplitudes, jnp.zeros_like(amplitudes))
    lowered = masked.astype(jnp.bfloat16)

    def ladder_one(channel):
        return jnp.dot(pair_interaction[channel], lowered[:, channel, :], preferred_element_type=jnp.float32)

    ladder = lax.map(ladder_one, jnp.arange(CHANNELS, dtype=jnp.int32))
    ladder = jnp.transpose(ladder, (1, 0, 2))
    blocks = masked.reshape(RT, TS, CHANNELS, HP // TC, TC)

    def cycle_one(index):
        chosen = ph_interaction[ph_owner[index]]
        return jnp.einsum("schk,chkl->schl", blocks[index], chosen, precision=lax.Precision.HIGHEST)

    cycle = lax.map(cycle_one, jnp.arange(RT, dtype=jnp.int32)).reshape(K, CHANNELS, HP)
    return jnp.where(live_mask[:, :, None], ladder, jnp.zeros_like(ladder)) + cycle
```

```python
import functools

import jax
import jax.numpy as jnp
from jax import lax
from jax.experimental import pallas as pl
from jax.experimental.pallas import tpu as pltpu
from jax.sharding import PartitionSpec as P

MESH = pl.DeviceIdType.MESH


def split(x):
    head = x.astype(jnp.bfloat16)
    return head, (x - head.astype(jnp.float32)).astype(jnp.bfloat16)


def kernel(
    dims,
    size_ref,
    owner_ref,
    amp_hbm,
    w_hbm,
    ph_hbm,
    out_hbm,
    amp,
    wbuf,
    low,
    part,
    sib_buf,
    x_send,
    x_recv,
    ph_all,
    out,
    amp_sem,
    w_sem,
    ph_sem,
    out_sem,
    sib_send_sem,
    sib_recv_sem,
    x_send_sem,
    x_recv_sem,
    z_send_sem,
    z_recv_sem,
    y_send_sem,
    y_recv_sem,
    p_send_sem,
    p_recv_sem,
):
    n_hi, n_chunk, chunk, rows, tile, tiles, per_owner = dims
    chan = lax.axis_index("chan")
    ctr = lax.axis_index("ctr")
    hi, lo = chan // 2, lax.rem(chan, 2)
    pair, core = ctr // 2, lax.rem(ctr, 2)
    half = per_owner // 2
    sibling = (chan, pair * 2 + 1 - core)
    across = (chan, (1 - pair) * 2 + core)
    beside = (hi * 2 + 1 - lo, ctr)

    def along(step):
        return (lax.rem(hi + step, n_hi) * 2 + lo, ctr)

    barrier = pltpu.get_barrier_semaphore()
    for device in (sibling, across, beside):
        pl.semaphore_signal(barrier, inc=1, device_id=device, device_id_type=MESH)

    @pl.loop(1, n_hi)
    def _(step):
        pl.semaphore_signal(barrier, inc=1, device_id=along(step), device_id_type=MESH)

    amp_copy = pltpu.make_async_copy(amp_hbm, amp, amp_sem)
    amp_copy.start()
    ph_copy = pltpu.make_async_copy(
        ph_hbm, ph_all.at[pl.ds(chan * per_owner, per_owner)], ph_sem
    )
    ph_copy.start()

    def w_copy(j, side):
        far = 1 - j // n_chunk
        owner_pair = pair + far * (1 - 2 * pair)
        owner_core = core + (1 - side) * (1 - 2 * core)
        start = (owner_pair * 2 + owner_core) * rows + lax.rem(j, n_chunk) * chunk
        return pltpu.make_async_copy(
            w_hbm.at[pl.ds(pl.multiple_of(start, chunk), chunk)],
            wbuf.at[j, pl.ds(side * chunk, chunk)],
            w_sem.at[j, side],
        )

    @pl.loop(0, 2 * n_chunk)
    def _(j):
        w_copy(j, 0).start()
        w_copy(j, 1).start()

    live = size_ref[0] * tile - ctr * rows

    def live_mask(start, count):
        return start + lax.broadcasted_iota(jnp.int32, (count, 128), 0) < live

    amp_copy.wait()

    @pl.loop(0, tiles)
    def _(r):
        mask = live_mask(r * tile, tile)
        for h in range(2):
            value = amp[pl.ds(r * 2 * tile + h, tile, 2), :]
            low[pl.ds(pl.multiple_of(r * tile, tile), tile), h * 128 : (h + 1) * 128] = (
                jnp.where(mask, value, jnp.zeros_like(value)).astype(jnp.bfloat16)
            )

    ph_copy.wait()
    pl.semaphore_wait(barrier, n_hi + 2)

    def ph_slot(owner, which):
        return ph_all.at[pl.ds(owner * per_owner + which * half, half)]

    def remote(ref, device, send_sem, recv_sem):
        return pltpu.make_async_remote_copy(
            src_ref=ref,
            dst_ref=ref,
            send_sem=send_sem,
            recv_sem=recv_sem,
            device_id=device,
            device_id_type=MESH,
        )

    def z_copy(step):
        return remote(ph_slot(chan, core), along(step), z_send_sem.at[step], z_recv_sem.at[step])

    def source(step):
        return lax.rem(hi + n_hi - step, n_hi)

    def y_copy(step):
        return remote(
            ph_slot(source(step) * 2 + lo, core), beside, y_send_sem.at[step], y_recv_sem.at[step]
        )

    def p_copy(step, other):
        owner = source(step) * 2 + lo + other * (1 - 2 * lo)
        return remote(
            ph_slot(owner, core), sibling, p_send_sem.at[other, step], p_recv_sem.at[other, step]
        )

    @pl.loop(1, n_hi)
    def _(step):
        z_copy(step).start()

    y_copy(0).start()

    def sib_copy(j):
        return pltpu.make_async_remote_copy(
            src_ref=part.at[j, pl.ds(0, chunk)],
            dst_ref=sib_buf.at[j],
            send_sem=sib_send_sem.at[j],
            recv_sem=sib_recv_sem.at[j],
            device_id=sibling,
            device_id_type=MESH,
        )

    def x_copy(i):
        return pltpu.make_async_remote_copy(
            src_ref=x_send.at[i],
            dst_ref=x_recv.at[i],
            send_sem=x_send_sem.at[i],
            recv_sem=x_recv_sem.at[i],
            device_id=across,
            device_id_type=MESH,
        )

    @pl.loop(0, 2 * n_chunk)
    def _(j):
        w_copy(j, 0).wait()
        w_copy(j, 1).wait()
        part[j] = jnp.dot(wbuf[j], low[...], preferred_element_type=jnp.float32)
        sib_copy(j).start()

        @pl.when((j >= 1) & (j <= n_chunk))
        def _():
            i = j - 1
            sib_copy(i).wait_recv()
            x_send[i] = (part[i, pl.ds(chunk, chunk)] + sib_buf[i]).astype(jnp.bfloat16)
            x_copy(i).start()

    @pl.loop(1, n_hi)
    def _(step):
        z_copy(step).wait_recv()
        y_copy(step).start()
        p_copy(step, 0).start()

    @pl.loop(0, n_hi)
    def _(step):
        y_copy(step).wait_recv()
        p_copy(step, 1).start()

    @pl.loop(1, n_hi)
    def _(step):
        p_copy(step, 0).wait_recv()

    @pl.loop(0, n_hi)
    def _(step):
        p_copy(step, 1).wait_recv()

    per_chunk = chunk // tile

    @pl.loop(0, n_chunk)
    def _(i):
        sib_copy(n_chunk + i).wait_recv()
        for t in range(per_chunk):
            r = i * per_chunk + t
            mask = live_mask(r * tile, tile)
            for h in range(2):
                cols = slice(h * 128, (h + 1) * 128)
                at = pl.ds(r * 2 * tile + h, tile, 2)
                value = amp[at, :]
                x_head, x_rest = split(jnp.where(mask, value, jnp.zeros_like(value)))
                m_head, m_rest = split(ph_all[owner_ref[h, r]])
                dot = functools.partial(jnp.dot, preferred_element_type=jnp.float32)
                cycle = dot(x_head, m_head) + (dot(x_rest, m_head) + dot(x_head, m_rest))
                ladder = (
                    part[n_chunk + i, chunk + t * tile : chunk + (t + 1) * tile, cols]
                    + sib_buf[n_chunk + i, t * tile : (t + 1) * tile, cols]
                )
                out[at, :] = jnp.where(mask, ladder, jnp.zeros_like(ladder)) + cycle

    def out_copy(i):
        window = pl.ds(pl.multiple_of(i * 2 * chunk, 2 * chunk), 2 * chunk)
        return pltpu.make_async_copy(out.at[window], out_hbm.at[window], out_sem.at[i])

    @pl.loop(0, n_chunk)
    def _(i):
        x_copy(i).wait_recv()
        for t in range(per_chunk):
            r = i * per_chunk + t
            mask = live_mask(r * tile, tile)
            for h in range(2):
                at = pl.ds(r * 2 * tile + h, tile, 2)
                far = x_recv[i, t * tile : (t + 1) * tile, h * 128 : (h + 1) * 128]
                far = far.astype(jnp.float32)
                out[at, :] += jnp.where(mask, far, jnp.zeros_like(far))
        out_copy(i).start()

    @pl.loop(0, 2 * n_chunk)
    def _(j):
        sib_copy(j).wait_send()

    @pl.loop(0, n_chunk)
    def _(i):
        x_copy(i).wait_send()

    @pl.loop(1, n_hi)
    def _(step):
        z_copy(step).wait_send()
        p_copy(step, 0).wait_send()

    @pl.loop(0, n_hi)
    def _(step):
        y_copy(step).wait_send()
        p_copy(step, 1).wait_send()

    @pl.loop(0, n_chunk)
    def _(i):
        out_copy(i).wait()


def local(n_chan, amplitudes, pair_interaction, ph_interaction, pp_size, ph_owner):
    rows, _, width = amplitudes.shape
    tiles = ph_owner.shape[0]
    per_owner, depth, _ = ph_interaction.shape
    whole_rows = pair_interaction.shape[1]
    tile = rows // tiles
    chunk = 3 * tile
    n_chunk = rows // chunk
    n_hi = n_chan // 2
    dims = (n_hi, n_chunk, chunk, rows, tile, tiles, per_owner)
    dma = pltpu.SemaphoreType.DMA
    any_space = pl.BlockSpec(memory_space=pl.ANY)
    smem = pl.BlockSpec(memory_space=pltpu.SMEM)
    result = pl.pallas_call(
        functools.partial(kernel, dims),
        out_shape=jax.ShapeDtypeStruct((2 * rows, 128), jnp.float32),
        in_specs=[smem, smem, any_space, any_space, any_space],
        out_specs=any_space,
        scratch_shapes=[
            pltpu.VMEM((2 * rows, 128), jnp.float32),
            pltpu.VMEM((2 * n_chunk, 2 * chunk, rows), jnp.bfloat16),
            pltpu.VMEM((rows, width), jnp.bfloat16),
            pltpu.VMEM((2 * n_chunk, 2 * chunk, width), jnp.float32),
            pltpu.VMEM((2 * n_chunk, chunk, width), jnp.float32),
            pltpu.VMEM((n_chunk, chunk, width), jnp.bfloat16),
            pltpu.VMEM((n_chunk, chunk, width), jnp.bfloat16),
            pltpu.VMEM((n_chan * per_owner, depth, depth), jnp.float32),
            pltpu.VMEM((2 * rows, 128), jnp.float32),
            dma,
            dma((2 * n_chunk, 2)),
            dma,
            dma((n_chunk,)),
            dma((2 * n_chunk,)),
            dma((2 * n_chunk,)),
            dma((n_chunk,)),
            dma((n_chunk,)),
            dma((n_hi,)),
            dma((n_hi,)),
            dma((n_hi,)),
            dma((n_hi,)),
            dma((2, n_hi)),
            dma((2, n_hi)),
        ],
        compiler_params=pltpu.CompilerParams(
            collective_id=0, has_side_effects=True, vmem_limit_bytes=48 * 1024 * 1024
        ),
        cost_estimate=pl.CostEstimate(
            flops=2 * whole_rows * rows * width,
            bytes_accessed=2 * whole_rows * rows + 8 * rows * width,
            transcendentals=0,
        ),
    )(
        pp_size,
        jnp.transpose(ph_owner, (1, 2, 0)).reshape(2, tiles),
        amplitudes.reshape(2 * rows, 128),
        pair_interaction.reshape(whole_rows, rows),
        ph_interaction,
    )
    return result.reshape(rows, 1, width)


def solution(mesh):
    in_specs = (
        P("ctr", "chan", None),
        P("chan", None, "ctr"),
        P("chan", None, None),
        P("chan"),
        P("ctr", "chan", None),
    )
    return jax.shard_map(
        functools.partial(local, mesh.shape["chan"]),
        mesh=mesh,
        in_specs=in_specs,
        out_specs=P("ctr", "chan", None),
        check_vma=False,
    )
```
